512 devices in a mesh: lon: 64 (over z, y), lat: 4 (over x_lo, core), lev: 2 (over x_hi).
Axes of the slice: x: 4 (x_hi: 2, x_lo: 2; x = x_hi * 2 + x_lo), y: 4, z: 16, core: 2. Of those that a mesh axis runs over, the one named last changes fastest.
Arguments:
- adjoint_in: float32 [32, 96, 8192], P('lev', 'lat', 'lon'), may hold values from -6 to 6
- cotangent: float32 [32, 96, 8192], P('lev', 'lat', 'lon'), may hold values from -3 to 5
- fraction: float32 [3, 32, 96, 8192], P(None, 'lev', 'lat', 'lon'), may hold values from 0 to 1
- base_index: int32 [32, 96, 8192], P('lev', 'lat', 'lon'), may hold values from 0 to 1523, as said below
- block_shift: int32 [2, 32, 96, 64], P(None, 'lev', 'lat', 'lon'), may hold values from -2 to 2, as said below
Outputs:
- adjoint_out: float32 [32, 96, 8192], P('lev', 'lat', 'lon')
The draws below stay inside these ranges and needn't reach their ends.
Inputs may be any that keep to these rules, and one draw needn't show every extreme that they name: `base_index`: an entry is e * 381 + c with level offset e from 0 to 3 and longitude position c from 0 to 380. `block_shift`: entry [0, l, J, b] is a longitude block offset of magnitude at most ((J // 24 + 1) * 2) // 4; entry [1, l, J, b] is a row offset from -2 to 1.
All inputs are finite; a program needn't handle non-finite values.
Results may differ from the reference program's by a relative error of at most 0.000054.
Values sent between devices are 32-bit elements; how exact they have to be, the bound alone decides.
No kernel may reach another device: no remote copies, remote signals or barrier semaphores. Data moves between devices by JAX's collectives and lax.ppermute only.
A program may use at most 64 MiB of HBM per device.

```python
import jax
import jax.numpy as jnp
from jax import lax

CLAT = 24
CLON = 128
KREACH = 3
LEVELS = 32
NLAT = 96
NLON = 8192
LONBLK = 64


def smooth_field(offset, amplitude):
    grid_shape = (LEVELS, NLAT, NLON)
    column_part = lax.broadcasted_iota(jnp.float32, grid_shape, 2) / NLON
    row_part = lax.broadcasted_iota(jnp.float32, grid_shape, 1) / NLAT
    return offset + amplitude * jnp.sin(6.283185307179586 * (column_part + row_part))


def draw_cotangent(key, part):
    key = jax.random.fold_in(key, 13)
    grid_shape = (LEVELS, NLAT, NLON)
    rough = jnp.clip(jax.random.normal(key, grid_shape, jnp.float32), -4.5, 4.5)
    values = smooth_field(0.9, 0.3) + 0.7 * rough
    return jnp.clip(values, -3.0, 5.0).astype(jnp.float32)


def draw_base_index(key, part):
    key = jax.random.fold_in(key, 11)
    first_key, second_key = jax.random.split(key)
    grid_shape = (LEVELS, NLAT, NLON)
    level_part = jax.random.randint(first_key, grid_shape, 0, 4)
    column_part = jax.random.randint(second_key, grid_shape, 0, 3 * CLON - 3)
    values = level_part * (3 * CLON - 3) + column_part
    values = values.at[0, 0, 0].set(12 * CLON - 13)
    values = values.at[0, 0, 1].set(0)
    return values.astype(jnp.int32)


def draw_block_shift(key, part):
    key = jax.random.fold_in(key, 12)
    first_key, second_key = jax.random.split(key)
    grid_shape = (LEVELS, NLAT, LONBLK)
    band_count = NLAT // CLAT
    row_band = lax.broadcasted_iota(jnp.int32, grid_shape, 1) // CLAT
    reach_limit = (row_band + 1) * (KREACH - 1) // band_count
    raw_bits = jax.random.randint(first_key, grid_shape, 0, 1 << 20)
    lon_shift = raw_bits % (2 * reach_limit + 1) - reach_limit
    lat_shift = jax.random.randint(second_key, grid_shape, -2, 2)
    lon_shift = lon_shift.at[0, NLAT - 1, 0].set(KREACH - 1)
    lon_shift = lon_shift.at[1, NLAT - 1, 0].set(1 - KREACH)
    lat_shift = lat_shift.at[0, 0, 0].set(-2)
    lat_shift = lat_shift.at[1, 0, 0].set(1)
    return jnp.stack([lon_shift, lat_shift]).astype(jnp.int32)


def steps_of(key, shape, cuts, smallest, top_value):
    loudness, own = 1.0, jax.random.fold_in(key, 6)
    for position, shards_of in cuts:
        steps = jnp.exp(jax.random.uniform(jax.random.fold_in(own, position), (shards_of,), jnp.float32, smallest / len(cuts), top_value / len(cuts)))
        loudness = loudness * jnp.repeat(steps, shape[position] // shards_of).reshape([-1 if axis == position else 1 for axis in range(len(shape))])
    return loudness


def gaussian(rng, dims, deviation, reach, cuts=(), dtype=jnp.bfloat16):
    result = jax.random.normal(rng, dims, jnp.float32) * deviation
    if len(cuts) > 0:
        result = steps_of(rng, dims, cuts, -0.22, 0.18) * result
    return jnp.clip(result, min=-reach, max=reach).astype(dtype)


def setup_inputs(seed: int = 0) -> dict:
    key_of = jax.random.split(jax.random.key(seed), 6)
    adjoint_in = gaussian(key_of[0], (LEVELS, NLAT, NLON), 1.0, 6.0, ((0, 2), (1, 4), (2, 64)), jnp.float32)
    cotangent = draw_cotangent(jax.random.fold_in(key_of[5], 71), 0)
    fraction = jnp.clip(1.0 * jax.random.uniform(key_of[2], (3, LEVELS, NLAT, NLON), jnp.float32) ** steps_of(key_of[2], (3, LEVELS, NLAT, NLON), ((1, 2), (2, 4), (3, 64)), -0.2, 0.2), 0.0, 1.0)
    base_index = draw_base_index(jax.random.fold_in(key_of[5], 71), 0)
    block_shift = draw_block_shift(jax.random.fold_in(key_of[5], 71), 0)
    return {"adjoint_in": adjoint_in, "cotangent": cotangent, "fraction": fraction, "base_index": base_index, "block_shift": block_shift}


def lagrange(fraction_part):
    less_one = fraction_part - 1.0
    less_two = fraction_part - 2.0
    plus_one = fraction_part + 1.0
    return (-fraction_part * less_one * less_two / 6.0,
            plus_one * less_one * less_two / 2.0,
            -plus_one * fraction_part * less_two / 2.0,
            plus_one * fraction_part * less_one / 6.0)


def reference(adjoint_in, cotangent, fraction, base_index, block_shift):
    stride = 3 * CLON - 3
    level_offset = base_index // stride
    column_offset = base_index - level_offset * stride
    grid_shape = base_index.shape
    level_grid = lax.broadcasted_iota(jnp.int32, grid_shape, 0)
    row_grid = lax.broadcasted_iota(jnp.int32, grid_shape, 1)
    column_grid = lax.broadcasted_iota(jnp.int32, grid_shape, 2)
    shifts = jnp.repeat(block_shift, CLON, axis=3)
    level_start = level_grid + level_offset
    row_start = row_grid + shifts[1] + 2
    column_start = (column_grid // CLON + shifts[0] - 1) * CLON + column_offset
    weights_level = lagrange(fraction[0])
    weights_row = lagrange(fraction[1])
    weights_column = lagrange(fraction[2])
    accumulated = jnp.zeros(((LEVELS + 6) * (NLAT + 6) * NLON,), jnp.float32)
    for level_tap in range(4):
        for row_tap in range(4):
            term_value = (cotangent * weights_level[level_tap]) * weights_row[row_tap]
            row_head = ((level_start + level_tap) * (NLAT + 6) + row_start + row_tap) * NLON
            for column_tap in range(4):
                flat_index = row_head + jnp.mod(column_start + column_tap, NLON)
                accumulated = accumulated.at[flat_index.reshape(-1)].add((term_value * weights_column[column_tap]).reshape(-1))
    accumulated = accumulated.reshape(LEVELS + 6, NLAT + 6, NLON)[3:3 + LEVELS, 3:3 + NLAT]
    return adjoint_in + accumulated
```

```python
import functools

import jax
import jax.numpy as jnp
from jax import lax
from jax.experimental import pallas as pl
from jax.experimental.pallas import tpu as pltpu
from jax.sharding import PartitionSpec as P

KREACH = 3
SPAN = 2 * KREACH + 1
HALO = 3
AXES = ("lon", "lat", "lev")
F32 = jnp.float32
BF16 = jnp.bfloat16


def lagrange(f):
    m1 = f - 1.0
    m2 = f - 2.0
    p1 = f + 1.0
    return (
        -f * m1 * m2 / 6.0,
        p1 * m1 * m2 / 2.0,
        -p1 * f * m2 / 2.0,
        p1 * f * m1 / 6.0,
    )


class Sizes:
    def __init__(self, levels, rows, cols):
        self.levels, self.rows, self.cols = levels, rows, cols
        self.nr = rows + 2 * HALO
        self.nl = -(-(levels + 2 * HALO + 1) // 8) * 8
        self.total = SPAN * self.nr * self.nl
        self.points = levels * rows


def prepare(sz, cot_ref, frac_ref, base_ref, pos_ref, wl_ref, wr_ref, wc_ref):
    stride = 3 * sz.cols - 3

    def body(l, carry):
        rows = pl.ds(pl.multiple_of(l * sz.rows, 8), sz.rows)
        base = base_ref[l]
        e = jnp.zeros_like(base)
        for cut in range(1, 4):
            e = e + (base >= cut * stride).astype(jnp.int32)
        c = base - e * stride
        q = c // sz.cols
        r = c - q * sz.cols
        pos_ref[0, rows] = e.astype(F32)
        pos_ref[1, rows] = q.astype(F32)
        pos_ref[2, rows] = r.astype(F32)
        cot = cot_ref[l]
        for t, w in enumerate(lagrange(frac_ref[0, l])):
            wl_ref[t, rows] = cot * w
        for t, w in enumerate(lagrange(frac_ref[1, l])):
            wr_ref[t, rows] = w
        for t, w in enumerate(lagrange(frac_ref[2, l])):
            high = w.astype(BF16).astype(F32)
            wc_ref[t, rows] = high
            wc_ref[4 + t, rows] = w - high
        return carry

    lax.fori_loop(0, sz.levels, body, 0)


def block_terms(sz, l, j, shift_ref, pos_ref, wl_ref, wr_ref, wc_ref):
    cols = sz.cols
    point = l * sz.rows + j

    def row(ref, t, n):
        return jnp.broadcast_to(ref[t, pl.ds(point, 1), :], (n, cols))

    def row16(ref, t):
        return row(ref, t, 16).astype(BF16)

    k8 = lax.broadcasted_iota(jnp.int32, (8, cols), 0).astype(F32)
    x16 = lax.broadcasted_iota(jnp.int32, (16, cols), 0).astype(F32).astype(BF16)
    z16 = jnp.zeros((16, cols), BF16)
    d = k8 - row(pos_ref, 0, 8)
    spread = jnp.zeros((8, cols), F32)
    for t in range(4):
        spread = jnp.where(d == float(t), row(wl_ref, t, 8), spread)
    term = jnp.concatenate([spread * row(wr_ref, t, 8) for t in range(4)], 0)
    high = term.astype(BF16)
    low = (term - high.astype(F32)).astype(BF16)
    q = row16(pos_ref, 1)
    q = jnp.concatenate([q, q], 0)
    z32 = jnp.zeros((32, cols), BF16)
    lh = jnp.concatenate([jnp.where(q == BF16(u), high, z32) for u in range(3)], 0)
    ll = jnp.concatenate([jnp.where(q == BF16(u), low, z32) for u in range(3)], 0)
    lhs = jnp.concatenate(
        [jnp.concatenate([lh, lh], 1), jnp.concatenate([ll, ll], 1)], 0
    )
    offset = x16 - row16(pos_ref, 2)
    wh = [row16(wc_ref, t) for t in range(4)]
    wl = [row16(wc_ref, 4 + t) for t in range(4)]
    bh, bl = [], []
    for tile in range(cols // 16 + 1):
        at = offset + BF16(16.0 * tile)
        a, b = z16, z16
        for t in range(4):
            hit = at == BF16(float(t))
            a = jnp.where(hit, wh[t], a)
            b = jnp.where(hit, wl[t], b)
        bh.append(a)
        bl.append(b)
    rest = [z16] * (cols // 16 - 1)
    band = jnp.concatenate(
        [jnp.concatenate(bh + rest, 0), jnp.concatenate(bl + rest, 0)], 1
    )
    out = lax.dot_general(
        lhs, band, (((1,), (1,)), ((), ())), preferred_element_type=F32
    )
    out = out[:96] + out[96:]
    blocks = shift_ref[l, j]
    shift = shift_ref[sz.levels + l, j]
    start = ((blocks + KREACH - 1) * sz.nr + (j + shift + 2)) * sz.nl + l
    return out[:, :cols], out[:64, cols:], start


def add_blocks(sz, places, acc_ref, *refs):
    results = [block_terms(sz, l, j, *refs) for l, j in places]
    for main, over, start in results:
        for q in range(3):
            for t in range(4):
                v = main[q * 32 + t * 8 : q * 32 + t * 8 + 8]
                if q > 0:
                    v = v + over[(q - 1) * 32 + t * 8 : (q - 1) * 32 + t * 8 + 8]
                at = pl.ds(start + (q * sz.nr + t) * sz.nl, 8)
                acc_ref[at] = acc_ref[at] + v


def clear_kernel(sz, acc_ref):
    zero = jnp.zeros((sz.nl, sz.cols), F32)

    def clear(i, carry):
        acc_ref[pl.ds(pl.multiple_of(i * sz.nl, 8), sz.nl)] = zero
        return carry

    lax.fori_loop(0, SPAN * sz.nr, clear, 0, unroll=6)


def first_kernel(
    sz, shift_ref, acc_in, cot_ref, frac_ref, base_ref,
    acc_ref, pos_ref, wl_ref, wr_ref, wc_ref, down_ref, up_ref,
):
    prepare(sz, cot_ref, frac_ref, base_ref, pos_ref, wl_ref, wr_ref, wc_ref)
    refs = (shift_ref, pos_ref, wl_ref, wr_ref, wc_ref)
    rim = list(range(HALO)) + list(range(sz.rows - HALO, sz.rows))

    def rims(i, carry):
        add_blocks(sz, [(i * 2 + u, j) for u in range(2) for j in rim], acc_ref, *refs)
        return carry

    lax.fori_loop(0, sz.levels // 2, rims, 0)
    edge = jnp.where(lax.axis_index("lev") == 0, sz.levels - HALO, 0)
    inner = range(HALO, sz.rows - HALO)

    def edges(i, carry):
        add_blocks(sz, [(edge + i, j) for j in inner], acc_ref, *refs)
        return carry

    lax.fori_loop(0, HALO, edges, 0)
    n = HALO * sz.nl
    for b in range(SPAN):
        down_ref[b] = acc_ref[pl.ds(b * sz.nr * sz.nl, n)]
        up_ref[b] = acc_ref[pl.ds((b * sz.nr + sz.rows + HALO) * sz.nl, n)]


def inner_kernel(
    sz, lower, upper, shift_ref, acc_in, pos_ref, wl_ref, wr_ref, wc_ref, acc_ref
):
    refs = (shift_ref, pos_ref, wl_ref, wr_ref, wc_ref)
    start = jnp.where(lax.axis_index("lev") == 0, 0, HALO)
    inner = range(HALO, sz.rows - HALO)

    def levels(i, carry):
        add_blocks(sz, [(start + i, j) for j in inner], acc_ref, *refs)
        return carry

    lax.fori_loop(lower, upper, levels, 0)


def row_kernel(sz, acc_in, down_ref, up_ref, acc_ref, out_ref):
    n = HALO * sz.nl
    slot = jnp.where(lax.axis_index("lev") == 0, sz.levels + HALO, 0)
    for b in range(SPAN):
        low = pl.ds((b * sz.nr + HALO) * sz.nl, n)
        high = pl.ds((b * sz.nr + sz.rows) * sz.nl, n)
        acc_ref[low] = acc_ref[low] + up_ref[b]
        acc_ref[high] = acc_ref[high] + down_ref[b]
    for b in range(SPAN):
        for k in range(HALO):
            for g in range(sz.rows // 8):
                at = (b * sz.nr + HALO + 8 * g) * sz.nl + slot + k
                out_ref[b, k, 8 * g : 8 * g + 8] = acc_ref[pl.ds(at, 8, stride=sz.nl)]


def level_kernel(sz, acc_ref, got_ref, *out_refs):
    target = jnp.where(lax.axis_index("lev") == 0, sz.levels - HALO, 0)
    for b in range(SPAN):
        def level(l, carry, b=b):
            for g in range(sz.rows // 8):
                at = (b * sz.nr + HALO + 8 * g) * sz.nl + HALO + l
                out_refs[b][l, 8 * g : 8 * g + 8] = acc_ref[pl.ds(at, 8, stride=sz.nl)]
            return carry

        lax.fori_loop(0, sz.levels, level, 0, unroll=4)
        for k in range(HALO):
            out_refs[b][target + k] = out_refs[b][target + k] + got_ref[b, k]


def call(kernel, out_shape, operands, flops, smem=0, aliases=None):
    vmem = pl.BlockSpec(memory_space=pltpu.VMEM)
    specs = []
    for i in range(len(operands)):
        if i < smem:
            specs.append(pl.BlockSpec(memory_space=pltpu.SMEM))
        else:
            specs.append(vmem)
    return pl.pallas_call(
        kernel,
        out_shape=out_shape,
        in_specs=specs,
        out_specs=jax.tree.map(lambda _: vmem, out_shape),
        input_output_aliases=aliases or {},
        cost_estimate=pl.CostEstimate(flops=flops, bytes_accessed=1 << 20, transcendentals=0),
        compiler_params=pltpu.CompilerParams(vmem_limit_bytes=32 << 20),
    )(*operands)


def shape(*dims):
    return jax.ShapeDtypeStruct(dims, F32)


def permute(value, sizes, step):
    pairs = []
    for lon in range(sizes[0]):
        for lat in range(sizes[1]):
            for lev in range(sizes[2]):
                to = step(lon, lat, lev)
                if to is not None:
                    pairs.append(
                        (
                            (lon * sizes[1] + lat) * sizes[2] + lev,
                            (to[0] * sizes[1] + to[1]) * sizes[2] + to[2],
                        )
                    )
    return lax.ppermute(value, AXES, pairs)


def local(adjoint_in, cotangent, fraction, base_index, block_shift):
    levels, rows, cols = cotangent.shape
    sz = Sizes(levels, rows, cols)
    sizes = tuple(lax.axis_size(axis) for axis in AXES)
    shifts = block_shift.reshape(2 * levels, rows)
    n = sz.points
    work = 2 * 192 * 256 * 256
    acc = call(functools.partial(clear_kernel, sz), shape(sz.total, cols), (), 10 * work)
    acc, pos, wl, wr, wc, down, up = call(
        functools.partial(first_kernel, sz),
        (
            shape(sz.total, cols), shape(3, n, cols), shape(4, n, cols),
            shape(4, n, cols), shape(8, n, cols),
            shape(SPAN, HALO * sz.nl, cols), shape(SPAN, HALO * sz.nl, cols),
        ),
        (shifts, acc, cotangent, fraction, base_index),
        150 * work,
        smem=1,
        aliases={1: 0},
    )

    def rows_by(d):
        def step(lon, lat, lev):
            return (lon, lat + d, lev) if 0 <= lat + d < sizes[1] else None
        return step

    got_down = permute(down, sizes, rows_by(-1))
    got_up = permute(up, sizes, rows_by(1))
    part = 5
    inner_levels = levels - HALO

    def inner(acc, lower, upper):
        return call(
            functools.partial(inner_kernel, sz, lower, upper),
            shape(sz.total, cols),
            (shifts, acc, pos, wl, wr, wc),
            (upper - lower) * 18 * work,
            smem=1,
            aliases={1: 0},
        )

    acc = inner(acc, 0, part)
    acc, edge = call(
        functools.partial(row_kernel, sz),
        (shape(sz.total, cols), shape(SPAN, HALO, rows, cols)),
        (acc, got_down, got_up),
        1 << 20,
        aliases={0: 0},
    )
    got_edge = permute(edge, sizes, lambda lon, lat, lev: (lon, lat, 1 - lev))
    acc = inner(acc, part, inner_levels)
    blocks = call(
        functools.partial(level_kernel, sz),
        tuple(shape(levels, rows, cols) for _ in range(SPAN)),
        (acc, got_edge),
        1 << 20,
    )

    def reach(lat):
        return ((lat + 1) * (KREACH - 1)) // sizes[1] + 1

    def around(d):
        def step(lon, lat, lev):
            far = max(reach(lat), reach(min(lat + 1, sizes[1] - 1)))
            return ((lon + d) % sizes[0], lat, lev) if abs(d) <= far else None

        return step

    total = adjoint_in + blocks[KREACH]
    order = (2, -2, 1, -1, 3, -3)
    got = [permute(blocks[KREACH + d], sizes, around(d)) for d in order]
    for value in got:
        total = total + value
    return total


def solution(mesh):
    return jax.shard_map(
        local,
        mesh=mesh,
        in_specs=(
            P("lev", "lat", "lon"),
            P("lev", "lat", "lon"),
            P(None, "lev", "lat", "lon"),
            P("lev", "lat", "lon"),
            P(None, "lev", "lat", "lon"),
        ),
        out_specs=P("lev", "lat", "lon"),
        check_vma=False,
    )
```

```python
import functools

import jax
import jax.numpy as jnp
from jax import lax
from jax.experimental import pallas as pl
from jax.experimental.pallas import tpu as pltpu
from jax.sharding import PartitionSpec as P

KREACH = 3
SPAN = 2 * KREACH + 1
HALO = 3
AXES = ("lon", "lat", "lev")
F32 = jnp.float32
BF16 = jnp.bfloat16


def lagrange(f):
    m1 = f - 1.0
    m2 = f - 2.0
    p1 = f + 1.0
    return (
        -f * m1 * m2 * (1.0 / 6.0),
        p1 * m1 * m2 * 0.5,
        -p1 * f * m2 * 0.5,
        p1 * f * m1 * (1.0 / 6.0),
    )


class Sizes:
    def __init__(self, levels, rows, cols):
        self.levels, self.rows, self.cols = levels, rows, cols
        self.nr = rows + 2 * HALO
        self.nl = -(-(levels + 2 * HALO + 1) // 8) * 8
        self.total = SPAN * self.nr * self.nl
        self.points = levels * rows


def prepare(sz, cot_ref, frac_ref, base_ref, pos_ref, wl_ref, wr_ref, wc_ref):
    stride = 3 * sz.cols - 3

    def body(l, carry):
        rows = pl.ds(pl.multiple_of(l * sz.rows, 8), sz.rows)
        base = base_ref[l]
        e = jnp.zeros_like(base)
        for cut in range(1, 4):
            e = e + (base >= cut * stride).astype(jnp.int32)
        c = base - e * stride
        q = (c >= sz.cols).astype(jnp.int32) + (c >= 2 * sz.cols).astype(jnp.int32)
        r = c - q * sz.cols
        pos_ref[0, rows] = e.astype(F32)
        pos_ref[1, rows] = q.astype(F32)
        part = r // 16
        pos_ref[2, rows] = (r - part * 16).astype(F32)
        pos_ref[3, rows] = part.astype(F32)
        cot = cot_ref[l]
        for t, w in enumerate(lagrange(frac_ref[0, l])):
            wl_ref[t, rows] = cot * w
        for t, w in enumerate(lagrange(frac_ref[1, l])):
            wr_ref[t, rows] = w
        for t, w in enumerate(lagrange(frac_ref[2, l])):
            high = w.astype(BF16).astype(F32)
            wc_ref[t, rows] = high
            wc_ref[4 + t, rows] = w - high
        return carry

    lax.fori_loop(0, sz.levels, body, 0)


def block_terms(sz, l, j, shift_ref, pos_ref, wl_ref, wr_ref, wc_ref):
    cols = sz.cols
    point = l * sz.rows + j

    def row(ref, t, n):
        return jnp.broadcast_to(ref[t, pl.ds(point, 1), :], (n, cols))

    def row16(ref, t):
        return row(ref, t, 16).astype(BF16)

    k8 = lax.broadcasted_iota(jnp.int32, (8, cols), 0).astype(F32)
    x16 = lax.broadcasted_iota(jnp.int32, (16, cols), 0).astype(F32).astype(BF16)
    z16 = jnp.zeros((16, cols), BF16)
    d = k8 - row(pos_ref, 0, 8)
    spread = jnp.zeros((8, cols), F32)
    for t in range(4):
        spread = jnp.where(d == float(t), row(wl_ref, t, 8), spread)
    term = jnp.concatenate([spread * row(wr_ref, t, 8) for t in range(4)], 0)
    high = term.astype(BF16)
    low = (term - high.astype(F32)).astype(BF16)
    q = row16(pos_ref, 1)
    q = jnp.concatenate([q, q], 0)
    z32 = jnp.zeros((32, cols), BF16)
    lh = jnp.concatenate([jnp.where(q == BF16(u), high, z32) for u in range(3)], 0)
    ll = jnp.concatenate([jnp.where(q == BF16(u), low, z32) for u in range(3)], 0)
    lhs = jnp.concatenate(
        [jnp.concatenate([lh, lh], 1), jnp.concatenate([ll, ll], 1)], 0
    )
    offset = x16 - row16(pos_ref, 2)
    below = offset < z16
    part = row16(pos_ref, 3)
    place = jnp.where(below, part + BF16(1.0), part)
    tap = jnp.where(below, offset + BF16(16.0), offset)
    wh, wl = z16, z16
    for t in range(4):
        hit = tap == BF16(float(t))
        wh = jnp.where(hit, row16(wc_ref, t), wh)
        wl = jnp.where(hit, row16(wc_ref, 4 + t), wl)
    bh, bl = [], []
    for tile in range(cols // 16 + 1):
        hit = place == BF16(float(tile))
        bh.append(jnp.where(hit, wh, z16))
        bl.append(jnp.where(hit, wl, z16))
    rest = [z16] * (cols // 16 - 1)
    band = jnp.concatenate(
        [jnp.concatenate(bh + rest, 0), jnp.concatenate(bl + rest, 0)], 1
    )
    out = lax.dot_general(
        lhs, band, (((1,), (1,)), ((), ())), preferred_element_type=F32
    )
    out = out[:96] + out[96:]
    blocks = shift_ref[l, j]
    shift = shift_ref[sz.levels + l, j]
    start = ((blocks + KREACH - 1) * sz.nr + (j + shift + 2)) * sz.nl + l
    return out[:, :cols], out[:64, cols:], start


def add_blocks(sz, places, acc_ref, *refs):
    def put(main, over, start):
        for q in range(3):
            for t in range(4):
                v = main[q * 32 + t * 8 : q * 32 + t * 8 + 8]
                if q > 0:
                    v = v + over[(q - 1) * 32 + t * 8 : (q - 1) * 32 + t * 8 + 8]
                at = pl.ds(start + (q * sz.nr + t) * sz.nl, 8)
                acc_ref[at] = acc_ref[at] + v

    waiting = None
    for l, j in places:
        found = block_terms(sz, l, j, *refs)
        if waiting is not None:
            put(*waiting)
        waiting = found
    put(*waiting)


def clear_kernel(sz, acc_ref):
    zero = jnp.zeros((sz.nl, sz.cols), F32)

    def clear(i, carry):
        acc_ref[pl.ds(pl.multiple_of(i * sz.nl, 8), sz.nl)] = zero
        return carry

    lax.fori_loop(0, SPAN * sz.nr, clear, 0, unroll=6)


def first_kernel(
    sz, shift_ref, acc_in, cot_ref, frac_ref, base_ref,
    acc_ref, pos_ref, wl_ref, wr_ref, wc_ref, near_ref, far_ref,
):
    prepare(sz, cot_ref, frac_ref, base_ref, pos_ref, wl_ref, wr_ref, wc_ref)
    refs = (shift_ref, pos_ref, wl_ref, wr_ref, wc_ref)
    rim = list(range(HALO)) + list(range(sz.rows - HALO, sz.rows))

    def rims(i, carry):
        add_blocks(sz, [(i * 4 + u, j) for u in range(4) for j in rim], acc_ref, *refs)
        return carry

    lax.fori_loop(0, sz.levels // 4, rims, 0)
    edge = jnp.where(lax.axis_index("lev") == 0, sz.levels - HALO, 0)
    inner = range(HALO, sz.rows - HALO)

    def edges(i, carry):
        add_blocks(sz, [(edge + i, j) for j in inner], acc_ref, *refs)
        return carry

    lax.fori_loop(0, HALO, edges, 0)
    n = HALO * sz.nl
    even = lax.axis_index("lat") % 2 == 0
    near = jnp.where(even, sz.rows + HALO, 0)
    far = jnp.where(even, 0, sz.rows + HALO)
    for b in range(SPAN):
        near_ref[b] = acc_ref[pl.ds((b * sz.nr + near) * sz.nl, n)]
        far_ref[b] = acc_ref[pl.ds((b * sz.nr + far) * sz.nl, n)]


def inner_kernel(
    sz, lower, upper, shift_ref, acc_in, pos_ref, wl_ref, wr_ref, wc_ref, acc_ref
):
    refs = (shift_ref, pos_ref, wl_ref, wr_ref, wc_ref)
    start = jnp.where(lax.axis_index("lev") == 0, 0, HALO)
    span = range(sz.levels - HALO)

    def rows(i, carry):
        places = [(start + l, HALO * (i + 1) + u) for u in range(HALO) for l in span]
        add_blocks(sz, places, acc_ref, *refs)
        return carry

    lax.fori_loop(lower, upper, rows, 0)


def row_kernel(sz, acc_in, near_ref, far_ref, acc_ref, out_ref):
    n = HALO * sz.nl
    slot = jnp.where(lax.axis_index("lev") == 0, sz.levels + HALO, 0)
    even = lax.axis_index("lat") % 2 == 0
    near_row = jnp.where(even, sz.rows, HALO)
    far_row = jnp.where(even, HALO, sz.rows)
    for b in range(SPAN):
        near = pl.ds((b * sz.nr + near_row) * sz.nl, n)
        acc_ref[near] = acc_ref[near] + near_ref[b]
        far = pl.ds((b * sz.nr + far_row) * sz.nl, n)
        acc_ref[far] = acc_ref[far] + far_ref[b]
    for b in range(SPAN):
        for k in range(HALO):
            for g in range(sz.rows // 8):
                at = (b * sz.nr + HALO + 8 * g) * sz.nl + slot + k
                out_ref[b, k, 8 * g : 8 * g + 8] = acc_ref[pl.ds(at, 8, stride=sz.nl)]


def level_kernel(sz, far_of, acc_ref, got_ref, *refs):
    out_refs, rim_refs = refs[:SPAN], refs[SPAN:]
    target = jnp.where(lax.axis_index("lev") == 0, sz.levels - HALO, 0)

    def cells(b, l, g):
        at = (b * sz.nr + HALO + 8 * g) * sz.nl + HALO + l
        return acc_ref[pl.ds(at, 8, stride=sz.nl)]

    for b in range(SPAN):
        def level(l, carry, b=b):
            for g in range(sz.rows // 8):
                out_refs[b][l, 8 * g : 8 * g + 8] = cells(b, l, g)
            return carry

        lax.fori_loop(0, sz.levels, level, 0, unroll=4)
        for k in range(HALO):
            out_refs[b][target + k] = out_refs[b][target + k] + got_ref[b, k]
    lat = lax.axis_index("lat")
    far = jnp.int32(KREACH)
    for i, d in enumerate(far_of):
        far = jnp.where(lat == i, d, far)
    last = sz.rows // 8 - 1
    for ref, b in zip(rim_refs, (KREACH + far, KREACH - far)):
        for l in range(sz.levels):
            ref[l] = cells(b, l, last)
        for k in range(HALO):
            ref[target + k] = ref[target + k] + got_ref[b, k, 8 * last : 8 * last + 8]


def call(kernel, out_shape, operands, flops, smem=0, aliases=None):
    vmem = pl.BlockSpec(memory_space=pltpu.VMEM)
    specs = []
    for i in range(len(operands)):
        if i < smem:
            specs.append(pl.BlockSpec(memory_space=pltpu.SMEM))
        else:
            specs.append(vmem)
    return pl.pallas_call(
        kernel,
        out_shape=out_shape,
        in_specs=specs,
        out_specs=jax.tree.map(lambda _: vmem, out_shape),
        input_output_aliases=aliases or {},
        cost_estimate=pl.CostEstimate(flops=flops, bytes_accessed=1 << 20, transcendentals=0),
        compiler_params=pltpu.CompilerParams(vmem_limit_bytes=32 << 20),
    )(*operands)


def shape(*dims):
    return jax.ShapeDtypeStruct(dims, F32)


def permute(value, sizes, step):
    pairs = []
    for lon in range(sizes[0]):
        for lat in range(sizes[1]):
            for lev in range(sizes[2]):
                to = step(lon, lat, lev)
                if to is not None:
                    pairs.append(
                        (
                            (lon * sizes[1] + lat) * sizes[2] + lev,
                            (to[0] * sizes[1] + to[1]) * sizes[2] + to[2],
                        )
                    )
    return lax.ppermute(value, AXES, pairs)


def local(adjoint_in, cotangent, fraction, base_index, block_shift):
    levels, rows, cols = cotangent.shape
    sz = Sizes(levels, rows, cols)
    sizes = tuple(lax.axis_size(axis) for axis in AXES)
    shifts = block_shift.reshape(2 * levels, rows)
    n = sz.points
    work = 2 * 192 * 256 * 256
    acc = call(functools.partial(clear_kernel, sz), shape(sz.total, cols), (), 10 * work)
    acc, pos, wl, wr, wc, near, far = call(
        functools.partial(first_kernel, sz),
        (
            shape(sz.total, cols), shape(4, n, cols), shape(4, n, cols),
            shape(4, n, cols), shape(8, n, cols),
            shape(SPAN, HALO * sz.nl, cols), shape(SPAN, HALO * sz.nl, cols),
        ),
        (shifts, acc, cotangent, fraction, base_index),
        150 * work,
        smem=1,
        aliases={1: 0},
    )

    def pair_with(odd):
        def step(lon, lat, lev):
            to = lat + 1 if lat % 2 == odd else lat - 1
            return (lon, to, lev) if 0 <= to < sizes[1] else None

        return step

    got_near = permute(near, sizes, pair_with(0))
    got_far = permute(far, sizes, pair_with(1))
    groups = (rows - 2 * HALO) // HALO

    def inner(acc, lower, upper):
        return call(
            functools.partial(inner_kernel, sz, lower, upper),
            shape(sz.total, cols),
            (shifts, acc, pos, wl, wr, wc),
            (upper - lower) * 39 * work,
            smem=1,
            aliases={1: 0},
        )

    acc = inner(acc, 0, groups // 2)
    acc, edge = call(
        functools.partial(row_kernel, sz),
        (shape(sz.total, cols), shape(SPAN, HALO, rows, cols)),
        (acc, got_near, got_far),
        1 << 20,
        aliases={0: 0},
    )
    got_edge = permute(edge, sizes, lambda lon, lat, lev: (lon, lat, 1 - lev))
    acc = inner(acc, groups // 2, groups)
    reach = [((lat + 1) * (KREACH - 1)) // sizes[1] + 1 for lat in range(sizes[1])]
    above = reach[1:] + reach[-1:]
    far_of = [r + 1 if nxt > r else 0 for r, nxt in zip(reach, above)]
    blocks = call(
        functools.partial(level_kernel, sz, far_of),
        tuple(shape(levels, rows, cols) for _ in range(SPAN))
        + tuple(shape(levels, 8, cols) for _ in range(2)),
        (acc, got_edge),
        1 << 20,
    )

    def around(d):
        def step(lon, lat, lev):
            return ((lon + d) % sizes[0], lat, lev) if abs(d) <= reach[lat] else None

        return step

    def rim_around(sign):
        def step(lon, lat, lev):
            d = sign * far_of[lat]
            return ((lon + d) % sizes[0], lat, lev) if d else None

        return step

    total = adjoint_in + blocks[KREACH]
    order = (2, -2, 1, -1, 3, -3)
    got = [permute(blocks[KREACH + d], sizes, around(d)) for d in order]
    rims = [permute(blocks[SPAN + i], sizes, rim_around(1 - 2 * i)) for i in range(2)]
    for value in got:
        total = total + value
    pads = ((0, 0), (rows - 8, 0), (0, 0))
    return total + jnp.pad(rims[0] + rims[1], pads)


def solution(mesh):
    return jax.shard_map(
        local,
        mesh=mesh,
        in_specs=(
            P("lev", "lat", "lon"),
            P("lev", "lat", "lon"),
            P(None, "lev", "lat", "lon"),
            P("lev", "lat", "lon"),
            P(None, "lev", "lat", "lon"),
        ),
        out_specs=P("lev", "lat", "lon"),
        check_vma=False,
    )
```

```python
import functools

import jax
import jax.numpy as jnp
from jax import lax
from jax.experimental import pallas as pl
from jax.experimental.pallas import tpu as pltpu
from jax.sharding import PartitionSpec as P

KREACH = 3
SPAN = 2 * KREACH + 1
HALO = 3
AXES = ("lon", "lat", "lev")
F32 = jnp.float32
BF16 = jnp.bfloat16


def lagrange(f):
    m1 = f - 1.0
    m2 = f - 2.0
    p1 = f + 1.0
    return (
        -f * m1 * m2 * (1.0 / 6.0),
        p1 * m1 * m2 * 0.5,
        -p1 * f * m2 * 0.5,
        p1 * f * m1 * (1.0 / 6.0),
    )


class Sizes:
    def __init__(self, levels, rows, cols):
        self.levels, self.rows, self.cols = levels, rows, cols
        self.nr = rows + 2 * HALO
        self.nl = -(-(levels + 2 * HALO + 1) // 8) * 8
        self.total = SPAN * self.nr * self.nl
        self.points = levels * rows


def prepare(sz, cot_ref, frac_ref, base_ref, pos_ref, wl_ref, wr_ref, wc_ref):
    stride = 3 * sz.cols - 3

    def body(l, carry):
        rows = pl.ds(pl.multiple_of(l * sz.rows, 8), sz.rows)
        base = base_ref[l]
        e = jnp.zeros_like(base)
        for cut in range(1, 4):
            e = e + (base >= cut * stride).astype(jnp.int32)
        c = base - e * stride
        q = (c >= sz.cols).astype(jnp.int32) + (c >= 2 * sz.cols).astype(jnp.int32)
        r = c - q * sz.cols
        pos_ref[0, rows] = e.astype(F32)
        pos_ref[1, rows] = q.astype(F32)
        part = r // 16
        pos_ref[2, rows] = (r - part * 16).astype(F32)
        pos_ref[3, rows] = part.astype(F32)
        cot = cot_ref[l]
        for t, w in enumerate(lagrange(frac_ref[0, l])):
            wl_ref[t, rows] = cot * w
        for t, w in enumerate(lagrange(frac_ref[1, l])):
            wr_ref[t, rows] = w
        for t, w in enumerate(lagrange(frac_ref[2, l])):
            high = w.astype(BF16).astype(F32)
            wc_ref[t, rows] = high
            wc_ref[4 + t, rows] = w - high
        return carry

    lax.fori_loop(0, sz.levels, body, 0)


def block_terms(sz, l, j, shift_ref, pos_ref, wl_ref, wr_ref, wc_ref):
    cols = sz.cols
    point = l * sz.rows + j

    def row(ref, t, n):
        return jnp.broadcast_to(ref[t, pl.ds(point, 1), :], (n, cols))

    def row16(ref, t):
        return row(ref, t, 16).astype(BF16)

    k8 = lax.broadcasted_iota(jnp.int32, (8, cols), 0).astype(F32)
    x16 = lax.broadcasted_iota(jnp.int32, (16, cols), 0).astype(F32).astype(BF16)
    z16 = jnp.zeros((16, cols), BF16)
    d = k8 - row(pos_ref, 0, 8)
    spread = jnp.zeros((8, cols), F32)
    for t in range(4):
        spread = jnp.where(d == float(t), row(wl_ref, t, 8), spread)
    term = jnp.concatenate([spread * row(wr_ref, t, 8) for t in range(4)], 0)
    high = term.astype(BF16)
    low = (term - high.astype(F32)).astype(BF16)
    q = row16(pos_ref, 1)
    q = jnp.concatenate([q, q], 0)
    z32 = jnp.zeros((32, cols), BF16)
    lh = jnp.concatenate([jnp.where(q == BF16(u), high, z32) for u in range(3)], 0)
    ll = jnp.concatenate([jnp.where(q == BF16(u), low, z32) for u in range(3)], 0)
    lhs = jnp.concatenate(
        [jnp.concatenate([lh, lh], 1), jnp.concatenate([ll, ll], 1)], 0
    )
    offset = x16 - row16(pos_ref, 2)
    below = offset < z16
    part = row16(pos_ref, 3)
    place = jnp.where(below, part + BF16(1.0), part)
    tap = jnp.where(below, offset + BF16(16.0), offset)
    wh, wl = z16, z16
    for t in range(4):
        hit = tap == BF16(float(t))
        wh = jnp.where(hit, row16(wc_ref, t), wh)
        wl = jnp.where(hit, row16(wc_ref, 4 + t), wl)
    bh, bl = [], []
    for tile in range(cols // 16 + 1):
        hit = place == BF16(float(tile))
        bh.append(jnp.where(hit, wh, z16))
        bl.append(jnp.where(hit, wl, z16))
    rest = [z16] * (cols // 16 - 1)
    band = jnp.concatenate(
        [jnp.concatenate(bh + rest, 0), jnp.concatenate(bl + rest, 0)], 1
    )
    out = lax.dot_general(
        lhs, band, (((1,), (1,)), ((), ())), preferred_element_type=F32
    )
    out = out[:96] + out[96:]
    blocks = shift_ref[l, j]
    shift = shift_ref[sz.levels + l, j]
    start = ((blocks + KREACH - 1) * sz.nr + (j + shift + 2)) * sz.nl + l
    return out[:, :cols], out[:64, cols:], start


def add_blocks(sz, places, acc_ref, *refs):
    def put(main, over, start):
        for q in range(3):
            for t in range(4):
                v = main[q * 32 + t * 8 : q * 32 + t * 8 + 8]
                if q > 0:
                    v = v + over[(q - 1) * 32 + t * 8 : (q - 1) * 32 + t * 8 + 8]
                at = pl.ds(start + (q * sz.nr + t) * sz.nl, 8)
                acc_ref[at] = acc_ref[at] + v

    waiting = None
    for l, j in places:
        found = block_terms(sz, l, j, *refs)
        if waiting is not None:
            put(*waiting)
        waiting = found
    put(*waiting)


def clear_kernel(sz, acc_ref):
    zero = jnp.zeros((sz.nl, sz.cols), F32)

    def clear(i, carry):
        acc_ref[pl.ds(pl.multiple_of(i * sz.nl, 8), sz.nl)] = zero
        return carry

    lax.fori_loop(0, SPAN * sz.nr, clear, 0, unroll=6)


def first_kernel(
    sz, shift_ref, acc_in, cot_ref, frac_ref, base_ref,
    acc_ref, pos_ref, wl_ref, wr_ref, wc_ref, near_ref, far_ref,
):
    prepare(sz, cot_ref, frac_ref, base_ref, pos_ref, wl_ref, wr_ref, wc_ref)
    refs = (shift_ref, pos_ref, wl_ref, wr_ref, wc_ref)
    rim = list(range(HALO)) + list(range(sz.rows - HALO, sz.rows))

    def rims(i, carry):
        add_blocks(sz, [(i * 4 + u, j) for u in range(4) for j in rim], acc_ref, *refs)
        return carry

    lax.fori_loop(0, sz.levels // 4, rims, 0)
    n = HALO * sz.nl
    even = lax.axis_index("lat") % 2 == 0
    near = jnp.where(even, sz.rows + HALO, 0)
    far = jnp.where(even, 0, sz.rows + HALO)
    for b in range(SPAN):
        near_ref[b] = acc_ref[pl.ds((b * sz.nr + near) * sz.nl, n)]
        far_ref[b] = acc_ref[pl.ds((b * sz.nr + far) * sz.nl, n)]


def inner_kernel(
    sz, lower, upper, shift_ref, acc_in, pos_ref, wl_ref, wr_ref, wc_ref, acc_ref
):
    refs = (shift_ref, pos_ref, wl_ref, wr_ref, wc_ref)
    start = jnp.where(lax.axis_index("lev") == 0, 0, HALO)
    edge = jnp.where(lax.axis_index("lev") == 0, sz.levels - HALO, 0)
    across = range(HALO, sz.rows - HALO)

    def edges(i, carry):
        add_blocks(sz, [(edge + i, j) for j in across], acc_ref, *refs)
        return carry

    if lower == 0:
        lax.fori_loop(0, HALO, edges, 0)
    span = range(sz.levels - HALO)

    def rows(i, carry):
        places = [(start + l, HALO * (i + 1) + u) for u in range(HALO) for l in span]
        add_blocks(sz, places, acc_ref, *refs)
        return carry

    lax.fori_loop(lower, upper, rows, 0)


def row_kernel(sz, acc_in, near_ref, far_ref, acc_ref, out_ref):
    n = HALO * sz.nl
    slot = jnp.where(lax.axis_index("lev") == 0, sz.levels + HALO, 0)
    even = lax.axis_index("lat") % 2 == 0
    near_row = jnp.where(even, sz.rows, HALO)
    far_row = jnp.where(even, HALO, sz.rows)
    for b in range(SPAN):
        near = pl.ds((b * sz.nr + near_row) * sz.nl, n)
        acc_ref[near] = acc_ref[near] + near_ref[b]
        far = pl.ds((b * sz.nr + far_row) * sz.nl, n)
        acc_ref[far] = acc_ref[far] + far_ref[b]
    for b in range(SPAN):
        for k in range(HALO):
            for g in range(sz.rows // 8):
                at = (b * sz.nr + HALO + 8 * g) * sz.nl + slot + k
                out_ref[b, k, 8 * g : 8 * g + 8] = acc_ref[pl.ds(at, 8, stride=sz.nl)]


def level_kernel(sz, far_of, acc_ref, got_ref, *refs):
    out_refs, rim_refs = refs[:SPAN], refs[SPAN:]
    target = jnp.where(lax.axis_index("lev") == 0, sz.levels - HALO, 0)

    def cells(b, l, g):
        at = (b * sz.nr + HALO + 8 * g) * sz.nl + HALO + l
        return acc_ref[pl.ds(at, 8, stride=sz.nl)]

    for b in range(SPAN):
        def level(l, carry, b=b):
            for g in range(sz.rows // 8):
                out_refs[b][l, 8 * g : 8 * g + 8] = cells(b, l, g)
            return carry

        lax.fori_loop(0, sz.levels, level, 0, unroll=4)
        for k in range(HALO):
            out_refs[b][target + k] = out_refs[b][target + k] + got_ref[b, k]
    lat = lax.axis_index("lat")
    far = jnp.int32(KREACH)
    for i, d in enumerate(far_of):
        far = jnp.where(lat == i, d, far)
    last = sz.rows // 8 - 1
    for ref, b in zip(rim_refs, (KREACH + far, KREACH - far)):
        for l in range(sz.levels):
            ref[l] = cells(b, l, last)
        for k in range(HALO):
            ref[target + k] = ref[target + k] + got_ref[b, k, 8 * last : 8 * last + 8]


def call(kernel, out_shape, operands, flops, smem=0, aliases=None):
    vmem = pl.BlockSpec(memory_space=pltpu.VMEM)
    specs = []
    for i in range(len(operands)):
        if i < smem:
            specs.append(pl.BlockSpec(memory_space=pltpu.SMEM))
        else:
            specs.append(vmem)
    return pl.pallas_call(
        kernel,
        out_shape=out_shape,
        in_specs=specs,
        out_specs=jax.tree.map(lambda _: vmem, out_shape),
        input_output_aliases=aliases or {},
        cost_estimate=pl.CostEstimate(flops=flops, bytes_accessed=1 << 20, transcendentals=0),
        compiler_params=pltpu.CompilerParams(vmem_limit_bytes=32 << 20),
    )(*operands)


def shape(*dims):
    return jax.ShapeDtypeStruct(dims, F32)


def permute(value, sizes, step):
    pairs = []
    for lon in range(sizes[0]):
        for lat in range(sizes[1]):
            for lev in range(sizes[2]):
                to = step(lon, lat, lev)
                if to is not None:
                    pairs.append(
                        (
                            (lon * sizes[1] + lat) * sizes[2] + lev,
                            (to[0] * sizes[1] + to[1]) * sizes[2] + to[2],
                        )
                    )
    return lax.ppermute(value, AXES, pairs)


def local(adjoint_in, cotangent, fraction, base_index, block_shift):
    levels, rows, cols = cotangent.shape
    sz = Sizes(levels, rows, cols)
    sizes = tuple(lax.axis_size(axis) for axis in AXES)
    shifts = block_shift.reshape(2 * levels, rows)
    n = sz.points
    work = 2 * 192 * 256 * 256
    acc = call(functools.partial(clear_kernel, sz), shape(sz.total, cols), (), 10 * work)
    acc, pos, wl, wr, wc, near, far = call(
        functools.partial(first_kernel, sz),
        (
            shape(sz.total, cols), shape(4, n, cols), shape(4, n, cols),
            shape(4, n, cols), shape(8, n, cols),
            shape(SPAN, HALO * sz.nl, cols), shape(SPAN, HALO * sz.nl, cols),
        ),
        (shifts, acc, cotangent, fraction, base_index),
        96 * work,
        smem=1,
        aliases={1: 0},
    )

    def pair_with(odd):
        def step(lon, lat, lev):
            to = lat + 1 if lat % 2 == odd else lat - 1
            return (lon, to, lev) if 0 <= to < sizes[1] else None

        return step

    got_near = permute(near, sizes, pair_with(0))
    got_far = permute(far, sizes, pair_with(1))
    groups = (rows - 2 * HALO) // HALO

    def inner(acc, lower, upper):
        return call(
            functools.partial(inner_kernel, sz, lower, upper),
            shape(sz.total, cols),
            (shifts, acc, pos, wl, wr, wc),
            ((upper - lower) * 39 + (54 if lower == 0 else 0)) * work,
            smem=1,
            aliases={1: 0},
        )

    acc = inner(acc, 0, groups // 3)
    acc, edge = call(
        functools.partial(row_kernel, sz),
        (shape(sz.total, cols), shape(SPAN, HALO, rows, cols)),
        (acc, got_near, got_far),
        1 << 20,
        aliases={0: 0},
    )
    got_edge = permute(edge, sizes, lambda lon, lat, lev: (lon, lat, 1 - lev))
    acc = inner(acc, groups // 3, groups)
    reach = [((lat + 1) * (KREACH - 1)) // sizes[1] + 1 for lat in range(sizes[1])]
    above = reach[1:] + reach[-1:]
    far_of = [r + 1 if nxt > r else 0 for r, nxt in zip(reach, above)]
    blocks = call(
        functools.partial(level_kernel, sz, far_of),
        tuple(shape(levels, rows, cols) for _ in range(SPAN))
        + tuple(shape(levels, 8, cols) for _ in range(2)),
        (acc, got_edge),
        1 << 20,
    )

    def around(d):
        def step(lon, lat, lev):
            return ((lon + d) % sizes[0], lat, lev) if abs(d) <= reach[lat] else None

        return step

    def rim_around(sign):
        def step(lon, lat, lev):
            d = sign * far_of[lat]
            return ((lon + d) % sizes[0], lat, lev) if d else None

        return step

    total = adjoint_in + blocks[KREACH]
    order = (2, -2, 1, -1, 3, -3)
    got = [permute(blocks[KREACH + d], sizes, around(d)) for d in order]
    rims = [permute(blocks[SPAN + i], sizes, rim_around(1 - 2 * i)) for i in range(2)]
    for value in got:
        total = total + value
    pads = ((0, 0), (rows - 8, 0), (0, 0))
    return total + jnp.pad(rims[0] + rims[1], pads)


def solution(mesh):
    return jax.shard_map(
        local,
        mesh=mesh,
        in_specs=(
            P("lev", "lat", "lon"),
            P("lev", "lat", "lon"),
            P(None, "lev", "lat", "lon"),
            P("lev", "lat", "lon"),
            P(None, "lev", "lat", "lon"),
        ),
        out_specs=P("lev", "lat", "lon"),
        check_vma=False,
    )
```
